512 devices in a mesh: row: 16 (over z), col: 32 (over y, x, core).
Axes of the slice: x: 4, y: 4, z: 16, core: 2. Of those that a mesh axis runs over, the one named last changes fastest.
Arguments:
- inputs: bfloat16 [256, 8192], P('col', 'row'), may hold values from -6 to 6
- out_grad: bfloat16 [256, 8192], P('col', 'row'), may hold values from -6 to 6
- w_gate: bfloat16 [8192, 14336], P('row', 'col'), may hold values from -0.0625 to 0.0625
- w_up: bfloat16 [8192, 14336], P('row', 'col'), may hold values from -0.0625 to 0.0625
- w_down: bfloat16 [14336, 8192], P('col', 'row'), may hold values from -0.046875 to 0.046875
Outputs:
- grad_inputs: bfloat16 [256, 8192], P('col', 'row')
- grad_gate: bfloat16 [8192, 14336], P('row', 'col')
- grad_up: bfloat16 [8192, 14336], P('row', 'col')
- grad_down: bfloat16 [14336, 8192], P('col', 'row')
The draws below stay inside these ranges and needn't reach their ends.
All inputs are finite; a program needn't handle non-finite values.
Results may differ from the reference program's by a relative error of at most 0.0049.
Values may be sent and summed in bfloat16 or wider, within the bound.
No kernel may reach another device: no remote copies, remote signals or barrier semaphores. Data moves between devices by JAX's collectives and lax.ppermute only.
A program may use at most 64 MiB of HBM per device.

```python
import jax
import jax.numpy as jnp

D = 8192
FF = 14336
TOKENS = 256


def block_scale(own_key, extent, pieces, low, high):
    loudness = 1.0
    for axis_at, blocks in pieces:
        heights = jax.random.uniform(jax.random.fold_in(jax.random.fold_in(own_key, 6), axis_at), (blocks,), jnp.float32, low / len(pieces), high / len(pieces))
        loudness = loudness * jnp.repeat(jnp.exp(heights), extent[axis_at] // blocks).reshape((-1,) + (1,) * (len(extent) - 1 - axis_at))
    return loudness


def gaussian(own_key, shape, spread, bound, split=(), kind=jnp.bfloat16):
    drawn = jax.random.normal(own_key, shape, jnp.float32) * spread
    if len(split) > 0:
        drawn = block_scale(own_key, shape, split, -0.22, 0.18) * drawn
    return jnp.clip(drawn, min=-bound, max=bound).astype(kind)


def setup_inputs(seed: int = 0) -> dict:
    seeds = jax.random.split(jax.random.key(seed), 6)
    return {
        "inputs": gaussian(seeds[0], (TOKENS, D), 1.0, 6.0, ((0, 32), (1, 16))),
        "out_grad": gaussian(seeds[1], (TOKENS, D), 1.0, 6.0, ((0, 32), (1, 16))),
        "w_gate": gaussian(seeds[2], (D, FF), D ** -0.5, 0.0625, ((0, 16), (1, 32))),
        "w_up": gaussian(seeds[3], (D, FF), D ** -0.5, 0.0625, ((0, 16), (1, 32))),
        "w_down": gaussian(seeds[4], (FF, D), FF ** -0.5, 0.046875, ((0, 32), (1, 16))),
    }


def reference(inputs, out_grad, w_gate, w_up, w_down):
    gate = jnp.dot(inputs, w_gate, preferred_element_type=jnp.float32)
    up = jnp.dot(inputs, w_up, preferred_element_type=jnp.float32)
    hidden_grad = jnp.dot(out_grad, w_down.T, preferred_element_type=jnp.float32)
    sigmoid_gate = jax.nn.sigmoid(gate)
    activated = gate * sigmoid_gate
    hidden = (activated * up).astype(jnp.bfloat16)
    up_delta = (hidden_grad * activated).astype(jnp.bfloat16)
    gate_delta = (hidden_grad * up * sigmoid_gate * (1.0 + gate * (1.0 - sigmoid_gate))).astype(jnp.bfloat16)
    grad_down = jnp.dot(hidden.T, out_grad, preferred_element_type=jnp.float32).astype(jnp.bfloat16)
    grad_gate = jnp.dot(inputs.T, gate_delta, preferred_element_type=jnp.float32).astype(jnp.bfloat16)
    grad_up = jnp.dot(inputs.T, up_delta, preferred_element_type=jnp.float32).astype(jnp.bfloat16)
    grad_inputs = jnp.dot(gate_delta, w_gate.T, preferred_element_type=jnp.float32)
    grad_inputs = grad_inputs + jnp.dot(up_delta, w_up.T, preferred_element_type=jnp.float32)
    return grad_inputs.astype(jnp.bfloat16), grad_gate, grad_up, grad_down
```

```python
import jax
import jax.numpy as jnp
from jax import lax
from jax.sharding import PartitionSpec as P


def contract(left, right, left_dim, right_dim):
    return lax.dot_general(
        left, right, (((left_dim,), (right_dim,)), ((), ())), preferred_element_type=jnp.float32
    )


def activate(sums, width):
    gate = sums[:, :width]
    up = sums[:, width : 2 * width]
    hidden_grad = sums[:, 2 * width :]
    sigmoid_gate = jax.nn.sigmoid(gate)
    activated = gate * sigmoid_gate
    hidden = (activated * up).astype(jnp.bfloat16)
    up_delta = (hidden_grad * activated).astype(jnp.bfloat16)
    gate_delta = (hidden_grad * up * sigmoid_gate * (1.0 + gate * (1.0 - sigmoid_gate))).astype(
        jnp.bfloat16
    )
    return (hidden, gate_delta, up_delta)


def exchange_sum(partial, axis, pieces):
    blocks = partial.reshape(pieces, partial.shape[0] // pieces, partial.shape[1])
    blocks = lax.all_to_all(blocks, axis, 0, 0)
    return jnp.sum(blocks.astype(jnp.float32), axis=0)


def on_device(rows, cols, inputs, out_grad, w_gate, w_up, w_down):
    depth = inputs.shape[1]
    width = w_gate.shape[1]
    both = lax.all_gather(jnp.concatenate([inputs, out_grad], axis=1), "col", axis=0, tiled=True)
    full_in = both[:, :depth]
    full_grad = both[:, depth:]
    partial = jnp.concatenate(
        [
            contract(full_in, w_gate, 1, 0).astype(jnp.bfloat16),
            contract(full_in, w_up, 1, 0).astype(jnp.bfloat16),
            contract(full_grad, w_down, 1, 1).astype(jnp.bfloat16),
        ],
        axis=1,
    )
    sums = exchange_sum(partial, "row", rows)
    hidden, gate_delta, up_delta = activate(sums, width)
    pieces = lax.all_gather(
        jnp.concatenate([gate_delta, up_delta, hidden], axis=1), "row", axis=0, tiled=True
    )
    piece_gate = pieces[:, :width]
    piece_up = pieces[:, width : 2 * width]
    piece_hidden = pieces[:, 2 * width :]
    block_in = contract(piece_gate, w_gate, 1, 1) + contract(piece_up, w_up, 1, 1)
    grad_inputs = exchange_sum(block_in.astype(jnp.bfloat16), "col", cols)
    acc_gate = contract(full_in, piece_gate, 0, 0)
    acc_up = contract(full_in, piece_up, 0, 0)
    acc_down = contract(piece_hidden, full_grad, 0, 0)
    return (
        grad_inputs.astype(jnp.bfloat16),
        acc_gate.astype(jnp.bfloat16),
        acc_up.astype(jnp.bfloat16),
        acc_down.astype(jnp.bfloat16),
    )


def solution(mesh):
    in_specs = (P("col", "row"), P("col", "row"), P("row", "col"), P("row", "col"), P("col", "row"))
    out_specs = (P("col", "row"), P("row", "col"), P("row", "col"), P("col", "row"))

    def step(*arrays):
        return on_device(mesh.shape["row"], mesh.shape["col"], *arrays)

    return jax.shard_map(
        step, mesh=mesh, in_specs=in_specs, out_specs=out_specs, check_vma=False
    )
```

```python
import jax
import jax.numpy as jnp
from jax import lax
from jax.sharding import PartitionSpec as P


def contract(left, right, left_dim, right_dim):
    return lax.dot_general(
        left, right, (((left_dim,), (right_dim,)), ((), ())), preferred_element_type=jnp.float32
    )


def activate(sums, width):
    gate = sums[:, :width]
    up = sums[:, width : 2 * width]
    hidden_grad = sums[:, 2 * width :]
    sigmoid_gate = jax.nn.sigmoid(gate)
    activated = gate * sigmoid_gate
    hidden = (activated * up).astype(jnp.bfloat16)
    up_delta = (hidden_grad * activated).astype(jnp.bfloat16)
    gate_delta = (hidden_grad * up * sigmoid_gate * (1.0 + gate * (1.0 - sigmoid_gate))).astype(
        jnp.bfloat16
    )
    return (hidden, gate_delta, up_delta)


def exchange_sum(partial, axis, pieces):
    blocks = partial.reshape(pieces, partial.shape[0] // pieces, partial.shape[1])
    blocks = lax.all_to_all(blocks, axis, 0, 0)
    return jnp.sum(blocks.astype(jnp.float32), axis=0)


def spread(block, axis, pieces):
    copies = jnp.broadcast_to(block[None], (pieces, *block.shape))
    return lax.all_to_all(copies, axis, 0, 0).reshape(-1, block.shape[1])


def on_device(rows, cols, inputs, out_grad, w_gate, w_up, w_down):
    depth = inputs.shape[1]
    width = w_gate.shape[1]
    both = spread(jnp.concatenate([inputs, out_grad], axis=1), "col", cols)
    full_in = both[:, :depth]
    full_grad = both[:, depth:]
    partial = jnp.concatenate(
        [
            contract(full_in, w_gate, 1, 0).astype(jnp.bfloat16),
            contract(full_in, w_up, 1, 0).astype(jnp.bfloat16),
            contract(full_grad, w_down, 1, 1).astype(jnp.bfloat16),
        ],
        axis=1,
    )
    sums = exchange_sum(partial, "row", rows)
    hidden, gate_delta, up_delta = activate(sums, width)
    pieces = lax.all_gather(
        jnp.concatenate([gate_delta, up_delta, hidden], axis=1), "row", axis=0, tiled=True
    )
    piece_gate = pieces[:, :width]
    piece_up = pieces[:, width : 2 * width]
    block_in = contract(piece_gate, w_gate, 1, 1) + contract(piece_up, w_up, 1, 1)
    block_in, pieces = lax.optimization_barrier((block_in.astype(jnp.bfloat16), pieces))
    grad_inputs = exchange_sum(block_in, "col", cols)
    piece_gate = pieces[:, :width]
    piece_up = pieces[:, width : 2 * width]
    piece_hidden = pieces[:, 2 * width :]
    acc_gate = contract(full_in, piece_gate, 0, 0)
    acc_up = contract(full_in, piece_up, 0, 0)
    acc_down = contract(piece_hidden, full_grad, 0, 0)
    return (
        grad_inputs.astype(jnp.bfloat16),
        acc_gate.astype(jnp.bfloat16),
        acc_up.astype(jnp.bfloat16),
        acc_down.astype(jnp.bfloat16),
    )


def solution(mesh):
    in_specs = (P("col", "row"), P("col", "row"), P("row", "col"), P("row", "col"), P("col", "row"))
    out_specs = (P("col", "row"), P("row", "col"), P("row", "col"), P("col", "row"))

    def step(*arrays):
        return on_device(mesh.shape["row"], mesh.shape["col"], *arrays)

    return jax.shard_map(
        step, mesh=mesh, in_specs=in_specs, out_specs=out_specs, check_vma=False
    )
```

```python
import jax
import jax.numpy as jnp
from jax import lax
from jax.sharding import Mesh
from jax.sharding import PartitionSpec as P

LEAST = -100.0


def contract(left, right, left_dim, right_dim):
    return lax.dot_general(
        left, right, (((left_dim,), (right_dim,)), ((), ())), preferred_element_type=jnp.float32
    )


def activate(gate, up, hidden_grad):
    sigmoid_gate = jax.nn.sigmoid(gate)
    activated = gate * sigmoid_gate
    hidden = (activated * up).astype(jnp.bfloat16)
    up_delta = (hidden_grad * activated).astype(jnp.bfloat16)
    gate_delta = (hidden_grad * up * sigmoid_gate * (1.0 + gate * (1.0 - sigmoid_gate))).astype(
        jnp.bfloat16
    )
    return (hidden, gate_delta, up_delta)


def row_exponent(block):
    largest = jnp.max(jnp.abs(block), axis=1, keepdims=True).astype(jnp.float32)
    return jnp.ceil(jnp.log2(jnp.maximum(largest, 2.0**LEAST)))


def encode(gate, up, hidden_grad, exp_in, exp_grad, shift):
    scale_in = jnp.exp2(shift - exp_in)
    scale_grad = jnp.exp2(shift - exp_grad)
    return jnp.concatenate(
        [
            (gate * scale_in).astype(jnp.float16),
            (up * scale_in).astype(jnp.float16),
            (hidden_grad * scale_grad).astype(jnp.float16),
            exp_in.astype(jnp.float16),
            exp_grad.astype(jnp.float16),
        ],
        axis=1,
    )


def decode(blocks, width, shift):
    blocks = blocks.astype(jnp.float32)
    exp_in = blocks[:, :, 3 * width : 3 * width + 1]
    exp_grad = blocks[:, :, 3 * width + 1 :]
    scale_in = jnp.exp2(exp_in - shift)
    scale_grad = jnp.exp2(exp_grad - shift)
    gate = jnp.sum(blocks[:, :, :width] * scale_in, axis=0)
    up = jnp.sum(blocks[:, :, width : 2 * width] * scale_in, axis=0)
    hidden_grad = jnp.sum(blocks[:, :, 2 * width : 3 * width] * scale_grad, axis=0)
    return gate, up, hidden_grad, jnp.max(exp_in, axis=0), jnp.max(exp_grad, axis=0)


def exchange(array, axis, pieces):
    return lax.all_to_all(array.reshape(pieces, -1, array.shape[1]), axis, 0, 0)


def spread(block, axis, pieces):
    copies = jnp.broadcast_to(block[None], (pieces, *block.shape))
    return lax.all_to_all(copies, axis, 0, 0).reshape(-1, block.shape[1])


def on_device(near, cols, inputs, out_grad, w_gate, w_up, w_down):
    depth = inputs.shape[1]
    width = w_gate.shape[1]
    both = spread(jnp.concatenate([inputs, out_grad], axis=1), "col", cols)
    full_in = both[:, :depth]
    full_grad = both[:, depth:]
    partial = encode(
        contract(full_in, w_gate, 1, 0),
        contract(full_in, w_up, 1, 0),
        contract(full_grad, w_down, 1, 1),
        row_exponent(full_in),
        row_exponent(full_grad),
        9.0,
    )
    sums = decode(exchange(partial, "near", near), width, 9.0)
    sums = decode(lax.all_gather(encode(*sums, 7.0), "far", axis=0), width, 7.0)
    hidden, gate_delta, up_delta = activate(*sums[:3])
    pieces = spread(jnp.concatenate([gate_delta, up_delta, hidden], axis=1), "near", near)
    piece_gate = pieces[:, :width]
    piece_up = pieces[:, width : 2 * width]
    block_in = contract(piece_gate, w_gate, 1, 1) + contract(piece_up, w_up, 1, 1)
    block_in, pieces = lax.optimization_barrier((block_in.astype(jnp.bfloat16), pieces))
    grad_inputs = jnp.sum(exchange(block_in, "col", cols).astype(jnp.float32), axis=0)
    piece_gate = pieces[:, :width]
    piece_up = pieces[:, width : 2 * width]
    piece_hidden = pieces[:, 2 * width :]
    acc_gate = contract(full_in, piece_gate, 0, 0)
    acc_up = contract(full_in, piece_up, 0, 0)
    acc_down = contract(piece_hidden, full_grad, 0, 0)
    return (
        grad_inputs.astype(jnp.bfloat16),
        acc_gate.astype(jnp.bfloat16),
        acc_up.astype(jnp.bfloat16),
        acc_down.astype(jnp.bfloat16),
    )


def solution(mesh):
    rows, cols = mesh.shape["row"], mesh.shape["col"]
    near = 4
    split = Mesh(mesh.devices.reshape(rows // near, near, cols), ("far", "near", "col"))
    row = ("far", "near")
    in_specs = (P("col", row), P("col", row), P(row, "col"), P(row, "col"), P("col", row))
    out_specs = (P("col", row), P(row, "col"), P(row, "col"), P("col", row))

    def step(*arrays):
        return on_device(near, cols, *arrays)

    return jax.shard_map(
        step, mesh=split, in_specs=in_specs, out_specs=out_specs, check_vma=False
    )
```

```python
import jax
import jax.numpy as jnp
from jax import lax
from jax.experimental import pallas as pl
from jax.experimental.pallas import tpu as pltpu
from jax.sharding import Mesh
from jax.sharding import PartitionSpec as P

ROW = ("far", "pair")
LEAST = -100.0
SHIFT = 9.0
NOTE = 64


def contract(left, right, left_dim, right_dim):
    return lax.dot_general(
        left, right, (((left_dim,), (right_dim,)), ((), ())), preferred_element_type=jnp.float32
    )


def activate(gate, up, hidden_grad):
    sigmoid_gate = jax.nn.sigmoid(gate)
    activated = gate * sigmoid_gate
    hidden = (activated * up).astype(jnp.bfloat16)
    up_delta = (hidden_grad * activated).astype(jnp.bfloat16)
    gate_delta = (hidden_grad * up * sigmoid_gate * (1.0 + gate * (1.0 - sigmoid_gate))).astype(
        jnp.bfloat16
    )
    return (hidden, gate_delta, up_delta)


def exchange(array, axis, pieces):
    return lax.all_to_all(array.reshape(pieces, -1, array.shape[-1]), axis, 0, 0)


def spread(block, axis, pieces):
    copies = jnp.broadcast_to(block[None], (pieces, *block.shape))
    return lax.all_to_all(copies, axis, 0, 0).reshape(-1, block.shape[1])


def partial_kernel(both, w_gate, w_up, w_down, sent, kept):
    width, depth = w_gate.shape
    mine = lax.axis_index("pair") == 0
    notes = []
    for i, (w, side) in enumerate(((w_gate, 0), (w_up, 0), (w_down, 1))):
        x = both[:, side * depth : (side + 1) * depth]
        if i != 1:
            largest = jnp.max(jnp.abs(x).astype(jnp.float32), axis=0, keepdims=True)
            largest = jnp.max(largest, axis=1, keepdims=True)
            exp = jnp.ceil(jnp.log2(jnp.maximum(largest, 2.0**LEAST)))
            scale = jnp.exp2(SHIFT - exp)
            notes.append(jnp.broadcast_to(exp, (sent.shape[0], NOTE // 2)))
        part = contract(x, w[...], 1, 1).reshape(-1, 2, 8, width)
        even = part[:, 0].reshape(-1, width)
        odd = part[:, 1].reshape(-1, width)
        at = pl.ds(i * width, width)
        kept[:, at] = jnp.where(mine, even, odd)
        sent[:, at] = (jnp.where(mine, odd, even) * scale).astype(sent.dtype)
    sent[:, 3 * width :] = jnp.concatenate(notes, axis=1).astype(sent.dtype)


def partial_sums(both, w_gate, w_up, w_down):
    tokens, width = both.shape[0], w_gate.shape[0]
    return pl.pallas_call(
        partial_kernel,
        out_shape=(
            jax.ShapeDtypeStruct((tokens // 2, 3 * width + NOTE), jnp.float32),
            jax.ShapeDtypeStruct((tokens // 2, 3 * width), jnp.float32),
        ),
        in_specs=[pl.BlockSpec(memory_space=pltpu.VMEM)] * 4,
        out_specs=[pl.BlockSpec(memory_space=pltpu.VMEM)] * 2,
        compiler_params=pltpu.CompilerParams(vmem_limit_bytes=16 << 20),
        name="partial_sums",
    )(both, w_gate, w_up, w_down)


def fold_kernel(got, kept, out):
    theirs = got[1 - lax.axis_index("pair")]
    width = kept.shape[1] // 3
    at = 3 * width
    scale_in = jnp.exp2(theirs[:, at : at + 1] - SHIFT)
    scale_grad = jnp.exp2(theirs[:, at + NOTE // 2 : at + NOTE // 2 + 1] - SHIFT)
    column = lax.broadcasted_iota(jnp.int32, kept.shape, 1)
    scale = jnp.where(column < 2 * width, scale_in, scale_grad)
    out[...] = (kept[...] + theirs[:, :at] * scale).astype(out.dtype)


def fold(sent, kept):
    got = lax.all_gather(sent.astype(jnp.float16), "pair", axis=0).astype(jnp.float32)
    return pl.pallas_call(
        fold_kernel,
        out_shape=jax.ShapeDtypeStruct(kept.shape, jnp.bfloat16),
        in_specs=[pl.BlockSpec(memory_space=pltpu.VMEM)] * 2,
        out_specs=pl.BlockSpec(memory_space=pltpu.VMEM),
        compiler_params=pltpu.CompilerParams(vmem_limit_bytes=16 << 20),
        name="fold",
    )(got, kept)


def block_kernel(pieces, w_gate, w_up, out):
    width = w_gate.shape[0]
    total = contract(pieces[:, :width], w_gate[...], 1, 0)
    total += contract(pieces[:, width : 2 * width], w_up[...], 1, 0)
    out[...] = total.astype(out.dtype)


def block_inputs(pieces, w_gate, w_up):
    return pl.pallas_call(
        block_kernel,
        out_shape=jax.ShapeDtypeStruct((pieces.shape[0], w_gate.shape[1]), jnp.bfloat16),
        in_specs=[pl.BlockSpec(memory_space=pltpu.VMEM)] * 3,
        out_specs=pl.BlockSpec(memory_space=pltpu.VMEM),
        compiler_params=pltpu.CompilerParams(vmem_limit_bytes=16 << 20),
        name="block_inputs",
    )(pieces, w_gate, w_up)


def on_device(rows, cols, inputs, out_grad, w_gate, w_up, w_down):
    depth = inputs.shape[1]
    width = w_gate.shape[1]
    both = spread(jnp.concatenate([inputs, out_grad], axis=1), "col", cols)
    full_in = both[:, :depth]
    full_grad = both[:, depth:]
    partial = fold(*partial_sums(both, w_gate.T, w_up.T, w_down))
    blocks = exchange(partial, ROW, rows).astype(jnp.float32)
    sums = jnp.sum(blocks.reshape(rows // 2, 2, *blocks.shape[1:]), axis=0)
    sums = sums.reshape(-1, sums.shape[-1])
    hidden, gate_delta, up_delta = activate(
        sums[:, :width], sums[:, width : 2 * width], sums[:, 2 * width :]
    )
    pieces = lax.all_gather(
        jnp.concatenate([gate_delta, up_delta, hidden], axis=1), ROW, axis=0, tiled=True
    )
    block_in = block_inputs(pieces, w_gate.T, w_up.T)
    block_in, pieces = lax.optimization_barrier((block_in, pieces))
    grad_inputs = jnp.sum(exchange(block_in, "col", cols).astype(jnp.float32), axis=0)
    piece_gate = pieces[:, :width]
    piece_up = pieces[:, width : 2 * width]
    piece_hidden = pieces[:, 2 * width :]
    acc_gate = contract(full_in, piece_gate, 0, 0)
    acc_up = contract(full_in, piece_up, 0, 0)
    acc_down = contract(piece_hidden, full_grad, 0, 0)
    return (
        grad_inputs.astype(jnp.bfloat16),
        acc_gate.astype(jnp.bfloat16),
        acc_up.astype(jnp.bfloat16),
        acc_down.astype(jnp.bfloat16),
    )


def solution(mesh):
    rows, cols = mesh.shape["row"], mesh.shape["col"]
    split = Mesh(mesh.devices.reshape(rows // 2, 2, cols), (*ROW, "col"))
    in_specs = (P("col", ROW), P("col", ROW), P(ROW, "col"), P(ROW, "col"), P("col", ROW))
    out_specs = (P("col", ROW), P(ROW, "col"), P(ROW, "col"), P("col", ROW))

    def step(*arrays):
        return on_device(rows, cols, *arrays)

    return jax.shard_map(
        step, mesh=split, in_specs=in_specs, out_specs=out_specs, check_vma=False
    )
```

```python
import jax
import jax.numpy as jnp
from jax import lax
from jax.experimental import pallas as pl
from jax.experimental.pallas import tpu as pltpu
from jax.sharding import Mesh
from jax.sharding import PartitionSpec as P

ROW = ("far", "pair")
LEAST = -100.0
SHIFT = 9.0
PAIR_SHIFT = 8.0
NOTE = 64


def contract(left, right, left_dim, right_dim):
    return lax.dot_general(
        left, right, (((left_dim,), (right_dim,)), ((), ())), preferred_element_type=jnp.float32
    )


def activate(gate, up, hidden_grad):
    sigmoid_gate = jax.nn.sigmoid(gate)
    activated = gate * sigmoid_gate
    hidden = (activated * up).astype(jnp.bfloat16)
    up_delta = (hidden_grad * activated).astype(jnp.bfloat16)
    gate_delta = (hidden_grad * up * sigmoid_gate * (1.0 + gate * (1.0 - sigmoid_gate))).astype(
        jnp.bfloat16
    )
    return (hidden, gate_delta, up_delta)


def exchange(array, axis, pieces):
    return lax.all_to_all(array.reshape(pieces, -1, array.shape[-1]), axis, 0, 0)


def spread(block, axis, pieces):
    copies = jnp.broadcast_to(block[None], (pieces, *block.shape))
    return lax.all_to_all(copies, axis, 0, 0).reshape(-1, block.shape[1])


def partial_kernel(both, w_gate, w_up, w_down, sent, kept):
    width, depth = w_gate.shape
    mine = lax.axis_index("pair") == 0
    notes = []
    for i, (w, side) in enumerate(((w_gate, 0), (w_up, 0), (w_down, 1))):
        x = both[:, side * depth : (side + 1) * depth]
        if i != 1:
            largest = jnp.max(jnp.abs(x).astype(jnp.float32), axis=0, keepdims=True)
            largest = jnp.max(largest, axis=1, keepdims=True)
            exp = jnp.ceil(jnp.log2(jnp.maximum(largest, 2.0**LEAST)))
            scale = jnp.exp2(SHIFT - exp)
            notes.append(jnp.broadcast_to(exp, (sent.shape[0], NOTE // 2)))
        part = contract(x, w[...], 1, 1).reshape(-1, 2, 8, width)
        even = part[:, 0].reshape(-1, width)
        odd = part[:, 1].reshape(-1, width)
        at = pl.ds(i * width, width)
        kept[:, at] = jnp.where(mine, even, odd)
        sent[:, at] = jnp.where(mine, odd, even) * scale
    notes = jnp.concatenate(notes, axis=1)
    kept[:, 3 * width :] = notes
    sent[:, 3 * width :] = notes


def partial_sums(both, w_gate, w_up, w_down):
    tokens, width = both.shape[0], w_gate.shape[0]
    return pl.pallas_call(
        partial_kernel,
        out_shape=[jax.ShapeDtypeStruct((tokens // 2, 3 * width + NOTE), jnp.float32)] * 2,
        in_specs=[pl.BlockSpec(memory_space=pltpu.VMEM)] * 4,
        out_specs=[pl.BlockSpec(memory_space=pltpu.VMEM)] * 2,
        compiler_params=pltpu.CompilerParams(vmem_limit_bytes=16 << 20),
        name="partial_sums",
    )(both, w_gate, w_up, w_down)


def exponents(block):
    at = block.shape[-1] - NOTE
    return block[..., at : at + 1], block[..., at + NOTE // 2 : at + NOTE // 2 + 1]


def fold_kernel(got, kept, out):
    theirs, mine = got[1 - lax.axis_index("pair")], kept[...]
    at = mine.shape[1] - NOTE
    column = lax.broadcasted_iota(jnp.int32, (mine.shape[0], at), 1)
    grads = column >= 2 * (at // 3)
    got_in, got_grad = exponents(theirs)
    own_in, own_grad = exponents(mine)
    exp_in, exp_grad = jnp.maximum(got_in, own_in), jnp.maximum(got_grad, own_grad)
    scale = jnp.where(grads, jnp.exp2(got_grad - SHIFT), jnp.exp2(got_in - SHIFT))
    total = mine[:, :at] + theirs[:, :at] * scale
    scale = jnp.where(grads, jnp.exp2(PAIR_SHIFT - exp_grad), jnp.exp2(PAIR_SHIFT - exp_in))
    out[:, :at] = total * scale
    note = (mine.shape[0], NOTE // 2)
    out[:, at:] = jnp.concatenate(
        [jnp.broadcast_to(exp_in, note), jnp.broadcast_to(exp_grad, note)], axis=1
    )


def fold(sent, kept):
    got = lax.all_gather(sent.astype(jnp.float16), "pair", axis=0).astype(jnp.float32)
    return pl.pallas_call(
        fold_kernel,
        out_shape=jax.ShapeDtypeStruct(kept.shape, jnp.float32),
        in_specs=[pl.BlockSpec(memory_space=pltpu.VMEM)] * 2,
        out_specs=pl.BlockSpec(memory_space=pltpu.VMEM),
        compiler_params=pltpu.CompilerParams(vmem_limit_bytes=16 << 20),
        name="fold",
    )(got, kept)


def activate_kernel(blocks, out):
    width = (blocks.shape[2] - NOTE) // 3
    stride = out.shape[2] // 2
    for h in range(2):
        sums = [0.0, 0.0]
        for s in range(h, blocks.shape[0], 2):
            block = blocks[s]
            parts = block[:, : 2 * width], block[:, 2 * width : 3 * width]
            for i, exp in enumerate(exponents(block)):
                sums[i] += parts[i] * jnp.exp2(exp - PAIR_SHIFT)
        hidden, gate_delta, up_delta = activate(sums[0][:, :width], sums[0][:, width:], sums[1])
        pad = jnp.zeros((hidden.shape[0], stride - 3 * width), out.dtype)
        out[0, :, h * stride : (h + 1) * stride] = jnp.concatenate(
            [gate_delta, up_delta, hidden, pad], axis=1
        )


def activations(blocks):
    stride = -(-blocks.shape[2] // 128) * 128
    return pl.pallas_call(
        activate_kernel,
        out_shape=jax.ShapeDtypeStruct((1, blocks.shape[1], 2 * stride), jnp.bfloat16),
        in_specs=[pl.BlockSpec(memory_space=pltpu.VMEM)],
        out_specs=pl.BlockSpec(memory_space=pltpu.VMEM),
        compiler_params=pltpu.CompilerParams(vmem_limit_bytes=16 << 20),
        name="activations",
    )(blocks)


def piece(pieces, h, which, width):
    stride = pieces.shape[2] // 2
    at = h * stride + which * width
    return pieces[:, :, at : at + width].reshape(-1, width)


def block_kernel(pieces, w_gate, w_up, out):
    width = w_gate.shape[0]
    for h in range(2):
        total = contract(piece(pieces, h, 0, width), w_gate[...], 1, 0)
        total += contract(piece(pieces, h, 1, width), w_up[...], 1, 0)
        out[:, h] = total.reshape(out.shape[0], *out.shape[2:]).astype(out.dtype)


def block_inputs(pieces, w_gate, w_up):
    return pl.pallas_call(
        block_kernel,
        out_shape=jax.ShapeDtypeStruct(
            (pieces.shape[0], 2, pieces.shape[1], w_gate.shape[1]), jnp.bfloat16
        ),
        in_specs=[pl.BlockSpec(memory_space=pltpu.VMEM)] * 3,
        out_specs=pl.BlockSpec(memory_space=pltpu.VMEM),
        compiler_params=pltpu.CompilerParams(vmem_limit_bytes=16 << 20),
        name="block_inputs",
    )(pieces, w_gate, w_up)


def grad_kernel(both, pieces, grad_gate, grad_up, grad_down):
    width, depth = grad_gate.shape
    for which, side, out in ((0, 0, grad_gate), (1, 0, grad_up), (2, 1, grad_down)):
        total = None
        for h in range(2):
            x = both[:, h, :, side * depth : (side + 1) * depth].reshape(-1, depth)
            term = contract(piece(pieces, h, which, width), x, 0, 0)
            total = term if total is None else total + term
        out[...] = total.astype(out.dtype)


def weight_grads(both, pieces, width):
    depth = both.shape[1] // 2
    both = both.reshape(pieces.shape[0], 2, pieces.shape[1], 2 * depth)
    return pl.pallas_call(
        grad_kernel,
        out_shape=[jax.ShapeDtypeStruct((width, depth), jnp.bfloat16)] * 3,
        in_specs=[pl.BlockSpec(memory_space=pltpu.VMEM)] * 2,
        out_specs=[pl.BlockSpec(memory_space=pltpu.VMEM)] * 3,
        compiler_params=pltpu.CompilerParams(vmem_limit_bytes=16 << 20),
        cost_estimate=pl.CostEstimate(flops=6 * 256 * 448 * 512, bytes_accessed=4 << 20, transcendentals=0),
        name="weight_grads",
    )(both, pieces)


def sum_kernel(blocks, out):
    out[...] = jnp.sum(blocks[...].astype(jnp.float32), axis=0).astype(out.dtype)


def final_sum(blocks):
    return pl.pallas_call(
        sum_kernel,
        out_shape=jax.ShapeDtypeStruct(blocks.shape[1:], jnp.bfloat16),
        in_specs=[pl.BlockSpec(memory_space=pltpu.VMEM)],
        out_specs=pl.BlockSpec(memory_space=pltpu.VMEM),
        compiler_params=pltpu.CompilerParams(vmem_limit_bytes=16 << 20),
        name="final_sum",
    )(blocks)


def on_device(rows, cols, inputs, out_grad, w_gate, w_up, w_down):
    width = w_gate.shape[1]
    both = spread(jnp.concatenate([inputs, out_grad], axis=1), "col", cols)
    partial = fold(*partial_sums(both, w_gate.T, w_up.T, w_down))
    blocks = exchange(partial.astype(jnp.float16), ROW, rows).astype(jnp.float32)
    payload = activations(blocks)
    pieces = lax.all_gather(payload, ROW, axis=0, tiled=True)
    block_in = block_inputs(pieces, w_gate.T, w_up.T).reshape(both.shape[0], -1)
    block_in, pieces = lax.optimization_barrier((block_in, pieces))
    grad_inputs = final_sum(exchange(block_in, "col", cols))
    grad_gate, grad_up, grad_down = weight_grads(both, pieces, width)
    return (grad_inputs, grad_gate.T, grad_up.T, grad_down)


def solution(mesh):
    rows, cols = mesh.shape["row"], mesh.shape["col"]
    split = Mesh(mesh.devices.reshape(rows // 2, 2, cols), (*ROW, "col"))
    in_specs = (P("col", ROW), P("col", ROW), P(ROW, "col"), P(ROW, "col"), P("col", ROW))
    out_specs = (P("col", ROW), P(ROW, "col"), P(ROW, "col"), P("col", ROW))

    def step(*arrays):
        return on_device(rows, cols, *arrays)

    return jax.shard_map(
        step, mesh=split, in_specs=in_specs, out_specs=out_specs, check_vma=False
    )
```

```python
import jax
import jax.numpy as jnp
from jax import lax
from jax.experimental import pallas as pl
from jax.experimental.pallas import tpu as pltpu
from jax.sharding import Mesh
from jax.sharding import PartitionSpec as P

ROW = ("far", "pair")
COL = ("chip", "core")
SWAP = [(0, 1), (1, 0)]
LEAST = -100.0
SHIFT = 9.0
PAIR_SHIFT = 8.0
NOTE = 64


def contract(left, right, left_dim, right_dim):
    return lax.dot_general(
        left, right, (((left_dim,), (right_dim,)), ((), ())), preferred_element_type=jnp.float32
    )


def activate(gate, up, hidden_grad):
    sigmoid_gate = jax.nn.sigmoid(gate)
    activated = gate * sigmoid_gate
    hidden = (activated * up).astype(jnp.bfloat16)
    up_delta = (hidden_grad * activated).astype(jnp.bfloat16)
    gate_delta = (hidden_grad * up * sigmoid_gate * (1.0 + gate * (1.0 - sigmoid_gate))).astype(
        jnp.bfloat16
    )
    return (hidden, gate_delta, up_delta)


def exchange(array, axis, pieces):
    return lax.all_to_all(array.reshape(pieces, -1, array.shape[-1]), axis, 0, 0)


def partial_kernel(both, *refs):
    own, theirs, sent, kept = refs
    width, depth = own.shape[0] // 3, own.shape[1]
    same = lax.axis_index("pair") == lax.axis_index("core")
    notes = []
    for i, side in enumerate((0, 0, 1)):
        x = both[:, side * depth : (side + 1) * depth]
        if i != 1:
            largest = jnp.max(jnp.abs(x).astype(jnp.float32), axis=0, keepdims=True)
            largest = jnp.max(largest, axis=1, keepdims=True)
            exp = jnp.ceil(jnp.log2(jnp.maximum(largest, 2.0**LEAST)))
            scale = jnp.exp2(SHIFT - exp)
            notes.append(jnp.broadcast_to(exp, (sent.shape[0], NOTE // 2)))
        at = slice(i * width, (i + 1) * width)
        first = contract(x, own[at], 1, 1)
        second = contract(x, theirs[at], 1, 1)
        kept[:, at] = jnp.where(same, first, second)
        sent[:, at] = jnp.where(same, second, first) * scale
    notes = jnp.concatenate(notes, axis=1)
    kept[:, 3 * width :] = notes
    sent[:, 3 * width :] = notes


def partial_sums(both, own, theirs):
    tokens, width = both.shape[0], own.shape[0] // 3
    return pl.pallas_call(
        partial_kernel,
        out_shape=[jax.ShapeDtypeStruct((tokens, 3 * width + NOTE), jnp.float32)] * 2,
        in_specs=[pl.BlockSpec(memory_space=pltpu.VMEM)] * 3,
        out_specs=[pl.BlockSpec(memory_space=pltpu.VMEM)] * 2,
        compiler_params=pltpu.CompilerParams(vmem_limit_bytes=16 << 20),
        name="partial_sums",
    )(both, own, theirs)


def exponents(block):
    at = block.shape[-1] - NOTE
    return block[..., at : at + 1], block[..., at + NOTE // 2 : at + NOTE // 2 + 1]


def fold_kernel(got, kept, out):
    theirs, mine = got[1 - lax.axis_index("pair")], kept[...]
    at = mine.shape[1] - NOTE
    column = lax.broadcasted_iota(jnp.int32, (mine.shape[0], at), 1)
    grads = column >= 2 * (at // 3)
    got_in, got_grad = exponents(theirs)
    own_in, own_grad = exponents(mine)
    exp_in, exp_grad = jnp.maximum(got_in, own_in), jnp.maximum(got_grad, own_grad)
    scale = jnp.where(grads, jnp.exp2(got_grad - SHIFT), jnp.exp2(got_in - SHIFT))
    total = mine[:, :at] + theirs[:, :at] * scale
    scale = jnp.where(grads, jnp.exp2(PAIR_SHIFT - exp_grad), jnp.exp2(PAIR_SHIFT - exp_in))
    out[:, :at] = total * scale
    note = (mine.shape[0], NOTE // 2)
    out[:, at:] = jnp.concatenate(
        [jnp.broadcast_to(exp_in, note), jnp.broadcast_to(exp_grad, note)], axis=1
    )


def fold(sent, kept):
    got = lax.all_gather(sent.astype(jnp.float16), "pair", axis=0).astype(jnp.float32)
    return pl.pallas_call(
        fold_kernel,
        out_shape=jax.ShapeDtypeStruct(kept.shape, jnp.float32),
        in_specs=[pl.BlockSpec(memory_space=pltpu.VMEM)] * 2,
        out_specs=pl.BlockSpec(memory_space=pltpu.VMEM),
        compiler_params=pltpu.CompilerParams(vmem_limit_bytes=16 << 20),
        name="fold",
    )(got, kept)


def activate_kernel(blocks, out):
    width = (blocks.shape[2] - NOTE) // 3
    stride = out.shape[2] // 2
    for h in range(2):
        sums = [0.0, 0.0]
        for s in range(h, blocks.shape[0], 2):
            block = blocks[s]
            parts = block[:, : 2 * width], block[:, 2 * width : 3 * width]
            for i, exp in enumerate(exponents(block)):
                sums[i] += parts[i] * jnp.exp2(exp - PAIR_SHIFT)
        hidden, gate_delta, up_delta = activate(sums[0][:, :width], sums[0][:, width:], sums[1])
        pad = jnp.zeros((hidden.shape[0], stride - 3 * width), out.dtype)
        out[0, :, h * stride : (h + 1) * stride] = jnp.concatenate(
            [gate_delta, up_delta, hidden, pad], axis=1
        )


def activations(blocks):
    stride = -(-blocks.shape[2] // 128) * 128
    return pl.pallas_call(
        activate_kernel,
        out_shape=jax.ShapeDtypeStruct((1, blocks.shape[1], 2 * stride), jnp.bfloat16),
        in_specs=[pl.BlockSpec(memory_space=pltpu.VMEM)],
        out_specs=pl.BlockSpec(memory_space=pltpu.VMEM),
        compiler_params=pltpu.CompilerParams(vmem_limit_bytes=16 << 20),
        name="activations",
    )(blocks)


def piece(pieces, which, width):
    return pieces[:, :, which * width : (which + 1) * width].reshape(-1, width)


def of_core(pieces, core):
    stride = pieces.shape[2] // 2
    return pieces[:, :, pl.ds(pl.multiple_of(core * stride, 128), stride)]


def block_kernel(pieces, own, theirs, out):
    width = own.shape[0] // 3
    core = lax.axis_index("core")
    total = 0.0
    for c, weights in ((core, own), (1 - core, theirs)):
        part = of_core(pieces, c)
        total += contract(piece(part, 0, width), weights[:width], 1, 0)
        total += contract(piece(part, 1, width), weights[width : 2 * width], 1, 0)
    out[...] = total.astype(out.dtype)


def block_inputs(pieces, own, theirs):
    return pl.pallas_call(
        block_kernel,
        out_shape=jax.ShapeDtypeStruct(
            (pieces.shape[0] * pieces.shape[1], own.shape[1]), jnp.bfloat16
        ),
        in_specs=[pl.BlockSpec(memory_space=pltpu.VMEM)] * 3,
        out_specs=pl.BlockSpec(memory_space=pltpu.VMEM),
        compiler_params=pltpu.CompilerParams(vmem_limit_bytes=16 << 20),
        name="block_inputs",
    )(pieces, own, theirs)


def give_kernel(pieces, out):
    out[...] = of_core(pieces, 1 - lax.axis_index("core")).reshape(out.shape)


def given(pieces):
    shape = (pieces.shape[0] * pieces.shape[1], pieces.shape[2] // 2)
    return pl.pallas_call(
        give_kernel,
        out_shape=jax.ShapeDtypeStruct(shape, jnp.bfloat16),
        in_specs=[pl.BlockSpec(memory_space=pltpu.VMEM)],
        out_specs=pl.BlockSpec(memory_space=pltpu.VMEM),
        compiler_params=pltpu.CompilerParams(vmem_limit_bytes=16 << 20),
        name="given",
    )(pieces)


def grad_kernel(both, pieces, got, grad_gate, grad_up, grad_down):
    width, depth = grad_gate.shape
    core = lax.axis_index("core")
    mine = of_core(pieces, core)
    for which, side, out in ((0, 0, grad_gate), (1, 0, grad_up), (2, 1, grad_down)):
        units = slice(which * width, (which + 1) * width)
        features = slice(side * depth, (side + 1) * depth)
        total = contract(piece(mine, which, width), both[core, :, features], 0, 0)
        total += contract(got[1 - core, :, units], both[1 - core, :, features], 0, 0)
        out[...] = total.astype(out.dtype)


def weight_grads(both, pieces, got, width):
    depth = both.shape[2] // 2
    return pl.pallas_call(
        grad_kernel,
        out_shape=[jax.ShapeDtypeStruct((width, depth), jnp.bfloat16)] * 3,
        in_specs=[pl.BlockSpec(memory_space=pltpu.VMEM)] * 3,
        out_specs=[pl.BlockSpec(memory_space=pltpu.VMEM)] * 3,
        compiler_params=pltpu.CompilerParams(vmem_limit_bytes=16 << 20),
        cost_estimate=pl.CostEstimate(
            flops=24 * both.shape[1] * width * depth, bytes_accessed=4 << 20, transcendentals=0
        ),
        name="weight_grads",
    )(both, pieces, got)


def sum_kernel(blocks, out):
    out[...] = jnp.sum(blocks[...].astype(jnp.float32), axis=0).astype(out.dtype)


def final_sum(blocks):
    return pl.pallas_call(
        sum_kernel,
        out_shape=jax.ShapeDtypeStruct(blocks.shape[1:], jnp.bfloat16),
        in_specs=[pl.BlockSpec(memory_space=pltpu.VMEM)],
        out_specs=pl.BlockSpec(memory_space=pltpu.VMEM),
        compiler_params=pltpu.CompilerParams(vmem_limit_bytes=16 << 20),
        name="final_sum",
    )(blocks)


def on_device(rows, chips, inputs, out_grad, w_gate, w_up, w_down):
    width = w_gate.shape[1]
    own = jnp.concatenate([w_gate.T, w_up.T, w_down], axis=0)
    copies = jnp.concatenate([inputs, out_grad], axis=1)
    copies = jnp.broadcast_to(copies[None], (chips, *copies.shape))
    both = lax.all_to_all(copies, "chip", 0, 0).reshape(-1, copies.shape[2])
    theirs = lax.ppermute(own, "core", SWAP)
    partial = fold(*partial_sums(both, own, theirs))
    blocks = exchange(partial.astype(jnp.float16), ROW, rows)
    payload = activations(blocks.astype(jnp.float32))
    pieces = lax.all_gather(payload, ROW, axis=0, tiled=True)
    block_in = block_inputs(pieces, own, theirs)
    block_in, pieces = lax.optimization_barrier((block_in, pieces))
    block_in = exchange(block_in, "chip", chips)
    got = lax.all_gather(given(pieces), "core", axis=0)
    grads = weight_grads(lax.all_gather(both, "core", axis=0), pieces, got, width)
    block_in, grad_gate, grad_up, grad_down = lax.optimization_barrier((block_in, *grads))
    grad_inputs = final_sum(block_in)
    return (grad_inputs, grad_gate.T, grad_up.T, grad_down)


def solution(mesh):
    rows, cols = mesh.shape["row"], mesh.shape["col"]
    split = Mesh(mesh.devices.reshape(rows // 2, 2, cols // 2, 2), ROW + COL)
    in_specs = (P(COL, ROW), P(COL, ROW), P(ROW, COL), P(ROW, COL), P(COL, ROW))
    out_specs = (P(COL, ROW), P(ROW, COL), P(ROW, COL), P(COL, ROW))

    def step(*arrays):
        return on_device(rows, cols // 2, *arrays)

    return jax.shard_map(
        step, mesh=split, in_specs=in_specs, out_specs=out_specs, check_vma=False
    )
```

```python
import jax
import jax.numpy as jnp
from jax import lax
from jax.experimental import pallas as pl
from jax.experimental.pallas import tpu as pltpu
from jax.sharding import Mesh
from jax.sharding import PartitionSpec as P

ROW = ("far", "pair")
COL = ("chip", "core")
SWAP = [(0, 1), (1, 0)]
LEAST = -100.0
SHIFT = 9.0
PAIR_SHIFT = 8.0
NOTE = 64


def contract(left, right, left_dim, right_dim):
    return lax.dot_general(
        left, right, (((left_dim,), (right_dim,)), ((), ())), preferred_element_type=jnp.float32
    )


def activate(gate, up, hidden_grad):
    sigmoid_gate = jax.nn.sigmoid(gate)
    activated = gate * sigmoid_gate
    hidden = (activated * up).astype(jnp.bfloat16)
    up_delta = (hidden_grad * activated).astype(jnp.bfloat16)
    gate_delta = (hidden_grad * up * sigmoid_gate * (1.0 + gate * (1.0 - sigmoid_gate))).astype(
        jnp.bfloat16
    )
    return (hidden, gate_delta, up_delta)


def exchange(array, axis, pieces):
    return lax.all_to_all(array.reshape(pieces, -1, array.shape[-1]), axis, 0, 0)


def partial_kernel(both, *refs):
    own, theirs, sent, kept = refs
    width, depth = own.shape[0] // 3, own.shape[1]
    same = lax.axis_index("pair") == lax.axis_index("core")
    notes = []
    for i, side in enumerate((0, 0, 1)):
        x = both[:, side * depth : (side + 1) * depth]
        if i != 1:
            largest = jnp.max(jnp.abs(x).astype(jnp.float32), axis=0, keepdims=True)
            largest = jnp.max(largest, axis=1, keepdims=True)
            exp = jnp.ceil(jnp.log2(jnp.maximum(largest, 2.0**LEAST)))
            scale = jnp.exp2(SHIFT - exp)
            notes.append(jnp.broadcast_to(exp, (sent.shape[0], NOTE // 2)))
        at = slice(i * width, (i + 1) * width)
        first = contract(x, own[at], 1, 1)
        second = contract(x, theirs[at], 1, 1)
        kept[:, at] = jnp.where(same, first, second)
        sent[:, at] = jnp.where(same, second, first) * scale
    notes = jnp.concatenate(notes, axis=1)
    kept[:, 3 * width :] = notes
    sent[:, 3 * width :] = notes


def partial_sums(both, own, theirs):
    tokens, width = both.shape[0], own.shape[0] // 3
    return pl.pallas_call(
        partial_kernel,
        out_shape=[jax.ShapeDtypeStruct((tokens, 3 * width + NOTE), jnp.float32)] * 2,
        in_specs=[pl.BlockSpec(memory_space=pltpu.VMEM)] * 3,
        out_specs=[pl.BlockSpec(memory_space=pltpu.VMEM)] * 2,
        compiler_params=pltpu.CompilerParams(vmem_limit_bytes=16 << 20),
        name="partial_sums",
    )(both, own, theirs)


def exponents(block):
    at = block.shape[-1] - NOTE
    return block[..., at : at + 1], block[..., at + NOTE // 2 : at + NOTE // 2 + 1]


def fold_kernel(got, kept, out):
    parity, core = lax.axis_index("pair"), lax.axis_index("core")
    theirs, mine = got[jnp.where(core == 0, 1 - parity, parity)], kept[...]
    at = mine.shape[1] - NOTE
    column = lax.broadcasted_iota(jnp.int32, (mine.shape[0], at), 1)
    grads = column >= 2 * (at // 3)
    got_in, got_grad = exponents(theirs)
    own_in, own_grad = exponents(mine)
    exp_in, exp_grad = jnp.maximum(got_in, own_in), jnp.maximum(got_grad, own_grad)
    scale = jnp.where(grads, jnp.exp2(got_grad - SHIFT), jnp.exp2(got_in - SHIFT))
    total = mine[:, :at] + theirs[:, :at] * scale
    scale = jnp.where(grads, jnp.exp2(PAIR_SHIFT - exp_grad), jnp.exp2(PAIR_SHIFT - exp_in))
    out[:, :at] = total * scale
    note = (mine.shape[0], NOTE // 2)
    out[:, at:] = jnp.concatenate(
        [jnp.broadcast_to(exp_in, note), jnp.broadcast_to(exp_grad, note)], axis=1
    )


def neighbours(rows):
    return [(2 * z + c, 2 * ((z + (1 if z % 2 == c else -1)) % rows) + c) for z in range(rows) for c in range(2)]


def fold(sent, kept, rows):
    groups = sorted({tuple(sorted(p, key=lambda i: (i - (i % 2) * 2) % (2 * rows))) for p in neighbours(rows)})
    got = lax.all_gather(
        sent.astype(jnp.float16), (*ROW, "core"), axis=0, axis_index_groups=[list(g) for g in groups]
    )
    got = got.astype(jnp.float32)
    return pl.pallas_call(
        fold_kernel,
        out_shape=jax.ShapeDtypeStruct(kept.shape, jnp.float32),
        in_specs=[pl.BlockSpec(memory_space=pltpu.VMEM)] * 2,
        out_specs=pl.BlockSpec(memory_space=pltpu.VMEM),
        compiler_params=pltpu.CompilerParams(vmem_limit_bytes=16 << 20),
        name="fold",
    )(got, kept)


def activate_kernel(blocks, out):
    width = (blocks.shape[2] - NOTE) // 3
    stride = out.shape[2] // 2
    for h in range(2):
        sums = [0.0, 0.0]
        for s in range(h, blocks.shape[0], 2):
            block = blocks[s]
            parts = block[:, : 2 * width], block[:, 2 * width : 3 * width]
            for i, exp in enumerate(exponents(block)):
                sums[i] += parts[i] * jnp.exp2(exp - PAIR_SHIFT)
        hidden, gate_delta, up_delta = activate(sums[0][:, :width], sums[0][:, width:], sums[1])
        pad = jnp.zeros((hidden.shape[0], stride - 3 * width), out.dtype)
        out[0, :, h * stride : (h + 1) * stride] = jnp.concatenate(
            [gate_delta, up_delta, hidden, pad], axis=1
        )


def activations(blocks):
    stride = -(-blocks.shape[2] // 128) * 128
    return pl.pallas_call(
        activate_kernel,
        out_shape=jax.ShapeDtypeStruct((1, blocks.shape[1], 2 * stride), jnp.bfloat16),
        in_specs=[pl.BlockSpec(memory_space=pltpu.VMEM)],
        out_specs=pl.BlockSpec(memory_space=pltpu.VMEM),
        compiler_params=pltpu.CompilerParams(vmem_limit_bytes=16 << 20),
        name="activations",
    )(blocks)


def piece(pieces, which, width):
    return pieces[:, :, which * width : (which + 1) * width].reshape(-1, width)


def of_core(pieces, core):
    stride = pieces.shape[2] // 2
    return pieces[:, :, pl.ds(pl.multiple_of(core * stride, 128), stride)]


def block_kernel(pieces, own, theirs, out):
    width = own.shape[0] // 3
    core = lax.axis_index("core")
    total = 0.0
    for c, weights in ((core, own), (1 - core, theirs)):
        part = of_core(pieces, c)
        total += contract(piece(part, 0, width), weights[:width], 1, 0)
        total += contract(piece(part, 1, width), weights[width : 2 * width], 1, 0)
    out[...] = total.astype(out.dtype)


def block_inputs(pieces, own, theirs):
    return pl.pallas_call(
        block_kernel,
        out_shape=jax.ShapeDtypeStruct(
            (pieces.shape[0] * pieces.shape[1], own.shape[1]), jnp.bfloat16
        ),
        in_specs=[pl.BlockSpec(memory_space=pltpu.VMEM)] * 3,
        out_specs=pl.BlockSpec(memory_space=pltpu.VMEM),
        compiler_params=pltpu.CompilerParams(vmem_limit_bytes=16 << 20),
        name="block_inputs",
    )(pieces, own, theirs)


def give_kernel(pieces, out):
    out[...] = of_core(pieces, 1 - lax.axis_index("core")).reshape(out.shape)


def given(pieces):
    shape = (pieces.shape[0] * pieces.shape[1], pieces.shape[2] // 2)
    return pl.pallas_call(
        give_kernel,
        out_shape=jax.ShapeDtypeStruct(shape, jnp.bfloat16),
        in_specs=[pl.BlockSpec(memory_space=pltpu.VMEM)],
        out_specs=pl.BlockSpec(memory_space=pltpu.VMEM),
        compiler_params=pltpu.CompilerParams(vmem_limit_bytes=16 << 20),
        name="given",
    )(pieces)


def grad_kernel(both, pieces, got, *refs):
    outs, (hold, sems) = refs[:3], refs[3:]
    width, depth = outs[0].shape
    core = lax.axis_index("core")
    mine = of_core(pieces, core)
    stores = []
    for which, side in ((2, 1), (0, 0), (1, 0)):
        units = slice(which * width, (which + 1) * width)
        features = slice(side * depth, (side + 1) * depth)
        total = contract(piece(mine, which, width), both[core, :, features], 0, 0)
        total += contract(got[1 - core, :, units], both[1 - core, :, features], 0, 0)
        hold[which] = total.astype(hold.dtype)
        stores.append(pltpu.make_async_copy(hold.at[which], outs[which], sems.at[which]))
        stores[-1].start()
    for store in stores:
        store.wait()


def weight_grads(both, pieces, got, width):
    depth = both.shape[2] // 2
    return pl.pallas_call(
        grad_kernel,
        out_shape=[jax.ShapeDtypeStruct((width, depth), jnp.bfloat16)] * 3,
        in_specs=[pl.BlockSpec(memory_space=pltpu.VMEM)] * 3,
        out_specs=[pl.BlockSpec(memory_space=pl.ANY)] * 3,
        scratch_shapes=[
            pltpu.VMEM((3, width, depth), jnp.bfloat16),
            pltpu.SemaphoreType.DMA((3,)),
        ],
        compiler_params=pltpu.CompilerParams(vmem_limit_bytes=16 << 20),
        cost_estimate=pl.CostEstimate(
            flops=24 * both.shape[1] * width * depth, bytes_accessed=4 << 20, transcendentals=0
        ),
        name="weight_grads",
    )(both, pieces, got)


def sum_kernel(blocks, out):
    out[...] = jnp.sum(blocks[...].astype(jnp.float32), axis=0).astype(out.dtype)


def final_sum(blocks):
    return pl.pallas_call(
        sum_kernel,
        out_shape=jax.ShapeDtypeStruct(blocks.shape[1:], jnp.bfloat16),
        in_specs=[pl.BlockSpec(memory_space=pltpu.VMEM)],
        out_specs=pl.BlockSpec(memory_space=pltpu.VMEM),
        compiler_params=pltpu.CompilerParams(vmem_limit_bytes=16 << 20),
        name="final_sum",
    )(blocks)


def on_device(rows, chips, inputs, out_grad, w_gate, w_up, w_down):
    width = w_gate.shape[1]
    own = jnp.concatenate([w_gate.T, w_up.T, w_down], axis=0)
    copies = jnp.concatenate([inputs, out_grad], axis=1)
    copies = jnp.broadcast_to(copies[None], (chips, *copies.shape))
    both = lax.all_to_all(copies, "chip", 0, 0).reshape(-1, copies.shape[2])
    theirs = lax.ppermute(own, "core", SWAP)
    partial = fold(*partial_sums(both, own, theirs), rows)
    blocks = exchange(partial.astype(jnp.float16), ROW, rows)
    payload = activations(blocks.astype(jnp.float32))
    pieces = lax.all_gather(payload, ROW, axis=0, tiled=True)
    block_in = block_inputs(pieces, own, theirs)
    block_in, pieces, both = lax.optimization_barrier((block_in, pieces, both))
    block_in = exchange(block_in, "chip", chips)
    got = lax.all_gather(given(pieces), "core", axis=0)
    grads = weight_grads(lax.all_gather(both, "core", axis=0), pieces, got, width)
    block_in, grad_gate, grad_up, grad_down = lax.optimization_barrier((block_in, *grads))
    grad_inputs = final_sum(block_in)
    return (grad_inputs, grad_gate.T, grad_up.T, grad_down)


def solution(mesh):
    rows, cols = mesh.shape["row"], mesh.shape["col"]
    split = Mesh(mesh.devices.reshape(rows // 2, 2, cols // 2, 2), ROW + COL)
    in_specs = (P(COL, ROW), P(COL, ROW), P(ROW, COL), P(ROW, COL), P(COL, ROW))
    out_specs = (P(COL, ROW), P(ROW, COL), P(ROW, COL), P(COL, ROW))

    def step(*arrays):
        return on_device(rows, cols // 2, *arrays)

    return jax.shard_map(
        step, mesh=split, in_specs=in_specs, out_specs=out_specs, check_vma=False
    )
```

```python
import jax
import jax.numpy as jnp
from jax import lax
from jax.experimental import pallas as pl
from jax.experimental.pallas import tpu as pltpu
from jax.sharding import Mesh
from jax.sharding import PartitionSpec as P

ROW = ("far", "pair")
COL = ("chip", "core")
SWAP = [(0, 1), (1, 0)]
LEAST = -100.0
SHIFT = 9.0
PAIR_SHIFT = 8.0
NOTE = 64


def contract(left, right, left_dim, right_dim):
    return lax.dot_general(
        left, right, (((left_dim,), (right_dim,)), ((), ())), preferred_element_type=jnp.float32
    )


def activate(gate, up, hidden_grad):
    sigmoid_gate = jax.nn.sigmoid(gate)
    activated = gate * sigmoid_gate
    hidden = (activated * up).astype(jnp.bfloat16)
    up_delta = (hidden_grad * activated).astype(jnp.bfloat16)
    gate_delta = (hidden_grad * up * sigmoid_gate * (1.0 + gate * (1.0 - sigmoid_gate))).astype(
        jnp.bfloat16
    )
    return (hidden, gate_delta, up_delta)


def exchange(array, axis, pieces):
    return lax.all_to_all(array.reshape(pieces, -1, array.shape[-1]), axis, 0, 0)


def own_kernel(both, own, out):
    width, depth = own.shape[0] // 3, own.shape[1]
    for i, side in enumerate((0, 0, 1)):
        x = both[:, side * depth : (side + 1) * depth]
        at = slice(i * width, (i + 1) * width)
        out[:, at] = contract(x, own[at], 1, 1)


def other_kernel(both, theirs, firsts, sent, kept):
    depth = theirs.shape[1]
    width = theirs.shape[0] // 3
    same = lax.axis_index("pair") == lax.axis_index("core")
    notes = []
    for i, side in enumerate((0, 0, 1)):
        x = both[:, side * depth : (side + 1) * depth]
        if i != 1:
            largest = jnp.max(jnp.abs(x).astype(jnp.float32), axis=0, keepdims=True)
            largest = jnp.max(largest, axis=1, keepdims=True)
            exp = jnp.ceil(jnp.log2(jnp.maximum(largest, 2.0**LEAST)))
            scale = jnp.exp2(SHIFT - exp)
            notes.append(jnp.broadcast_to(exp, (sent.shape[0], NOTE // 2)))
        at = slice(i * width, (i + 1) * width)
        first = firsts[:, at]
        second = contract(x, theirs[at], 1, 1)
        kept[:, at] = jnp.where(same, first, second)
        sent[:, at] = jnp.where(same, second, first) * scale
    notes = jnp.concatenate(notes, axis=1)
    kept[:, 3 * width :] = notes
    sent[:, 3 * width :] = notes


def partial_sums(both, own, theirs):
    tokens, width = both.shape[0], own.shape[0] // 3
    vmem = pl.BlockSpec(memory_space=pltpu.VMEM)
    params = pltpu.CompilerParams(vmem_limit_bytes=16 << 20)
    firsts = pl.pallas_call(
        own_kernel,
        out_shape=jax.ShapeDtypeStruct((tokens, 3 * width), jnp.float32),
        in_specs=[vmem] * 2,
        out_specs=vmem,
        compiler_params=params,
        cost_estimate=pl.CostEstimate(flops=10**11, bytes_accessed=3 << 20, transcendentals=0),
        name="own_sums",
    )(both, own)
    return pl.pallas_call(
        other_kernel,
        out_shape=[jax.ShapeDtypeStruct((tokens, 3 * width + NOTE), jnp.float32)] * 2,
        in_specs=[vmem] * 3,
        out_specs=[vmem] * 2,
        compiler_params=params,
        name="other_sums",
    )(both, theirs, firsts)


def exponents(block):
    at = block.shape[-1] - NOTE
    return block[..., at : at + 1], block[..., at + NOTE // 2 : at + NOTE // 2 + 1]


def fold_kernel(got, kept, out):
    parity, core = lax.axis_index("pair"), lax.axis_index("core")
    theirs, mine = got[jnp.where(core == 0, 1 - parity, parity)], kept[...]
    at = mine.shape[1] - NOTE
    column = lax.broadcasted_iota(jnp.int32, (mine.shape[0], at), 1)
    grads = column >= 2 * (at // 3)
    got_in, got_grad = exponents(theirs)
    own_in, own_grad = exponents(mine)
    exp_in, exp_grad = jnp.maximum(got_in, own_in), jnp.maximum(got_grad, own_grad)
    scale = jnp.where(grads, jnp.exp2(got_grad - SHIFT), jnp.exp2(got_in - SHIFT))
    total = mine[:, :at] + theirs[:, :at] * scale
    scale = jnp.where(grads, jnp.exp2(PAIR_SHIFT - exp_grad), jnp.exp2(PAIR_SHIFT - exp_in))
    out[:, :at] = total * scale
    note = (mine.shape[0], NOTE // 2)
    out[:, at:] = jnp.concatenate(
        [jnp.broadcast_to(exp_in, note), jnp.broadcast_to(exp_grad, note)], axis=1
    )


def neighbours(rows):
    return [(2 * z + c, 2 * ((z + (1 if z % 2 == c else -1)) % rows) + c) for z in range(rows) for c in range(2)]


def fold(sent, kept, rows):
    groups = sorted({tuple(sorted(p, key=lambda i: (i - (i % 2) * 2) % (2 * rows))) for p in neighbours(rows)})
    got = lax.all_gather(
        sent.astype(jnp.float16), (*ROW, "core"), axis=0, axis_index_groups=[list(g) for g in groups]
    )
    got = got.astype(jnp.float32)
    return pl.pallas_call(
        fold_kernel,
        out_shape=jax.ShapeDtypeStruct(kept.shape, jnp.float32),
        in_specs=[pl.BlockSpec(memory_space=pltpu.VMEM)] * 2,
        out_specs=pl.BlockSpec(memory_space=pltpu.VMEM),
        compiler_params=pltpu.CompilerParams(vmem_limit_bytes=16 << 20),
        name="fold",
    )(got, kept)


def activate_kernel(blocks, out):
    width = (blocks.shape[2] - NOTE) // 3
    stride = out.shape[2] // 2
    for h in range(2):
        sums = [0.0, 0.0]
        for s in range(h, blocks.shape[0], 2):
            block = blocks[s]
            parts = block[:, : 2 * width], block[:, 2 * width : 3 * width]
            for i, exp in enumerate(exponents(block)):
                sums[i] += parts[i] * jnp.exp2(exp - PAIR_SHIFT)
        hidden, gate_delta, up_delta = activate(sums[0][:, :width], sums[0][:, width:], sums[1])
        pad = jnp.zeros((hidden.shape[0], stride - 3 * width), out.dtype)
        out[0, :, h * stride : (h + 1) * stride] = jnp.concatenate(
            [gate_delta, up_delta, hidden, pad], axis=1
        )


def activations(blocks):
    stride = -(-blocks.shape[2] // 128) * 128
    return pl.pallas_call(
        activate_kernel,
        out_shape=jax.ShapeDtypeStruct((1, blocks.shape[1], 2 * stride), jnp.bfloat16),
        in_specs=[pl.BlockSpec(memory_space=pltpu.VMEM)],
        out_specs=pl.BlockSpec(memory_space=pltpu.VMEM),
        compiler_params=pltpu.CompilerParams(vmem_limit_bytes=16 << 20),
        name="activations",
    )(blocks)


def piece(pieces, which, width):
    return pieces[:, :, which * width : (which + 1) * width].reshape(-1, width)


def of_core(pieces, core):
    stride = pieces.shape[2] // 2
    return pieces[:, :, pl.ds(pl.multiple_of(core * stride, 128), stride)]


def block_kernel(pieces, own, theirs, out):
    width = own.shape[0] // 3
    core = lax.axis_index("core")
    total = 0.0
    for c, weights in ((core, own), (1 - core, theirs)):
        part = of_core(pieces, c)
        total += contract(piece(part, 0, width), weights[:width], 1, 0)
        total += contract(piece(part, 1, width), weights[width : 2 * width], 1, 0)
    out[...] = total.astype(out.dtype)


def block_inputs(pieces, own, theirs):
    return pl.pallas_call(
        block_kernel,
        out_shape=jax.ShapeDtypeStruct(
            (pieces.shape[0] * pieces.shape[1], own.shape[1]), jnp.bfloat16
        ),
        in_specs=[pl.BlockSpec(memory_space=pltpu.VMEM)] * 3,
        out_specs=pl.BlockSpec(memory_space=pltpu.VMEM),
        compiler_params=pltpu.CompilerParams(vmem_limit_bytes=16 << 20),
        name="block_inputs",
    )(pieces, own, theirs)


def give_kernel(pieces, out):
    out[...] = of_core(pieces, 1 - lax.axis_index("core")).reshape(out.shape)


def given(pieces):
    shape = (pieces.shape[0] * pieces.shape[1], pieces.shape[2] // 2)
    return pl.pallas_call(
        give_kernel,
        out_shape=jax.ShapeDtypeStruct(shape, jnp.bfloat16),
        in_specs=[pl.BlockSpec(memory_space=pltpu.VMEM)],
        out_specs=pl.BlockSpec(memory_space=pltpu.VMEM),
        compiler_params=pltpu.CompilerParams(vmem_limit_bytes=16 << 20),
        name="given",
    )(pieces)


def grad_kernel(both, pieces, got, *refs):
    outs, (hold, sems) = refs[:3], refs[3:]
    width, depth = outs[0].shape
    core = lax.axis_index("core")
    mine = of_core(pieces, core)
    stores = []
    for which, side in ((2, 1), (0, 0), (1, 0)):
        units = slice(which * width, (which + 1) * width)
        features = slice(side * depth, (side + 1) * depth)
        delta = jnp.concatenate([piece(mine, which, width), got[1 - core, :, units]], axis=0)
        x = jnp.concatenate([both[core, :, features], both[1 - core, :, features]], axis=0)
        total = contract(delta, x, 0, 0)
        hold[which] = total.astype(hold.dtype)
        stores.append(pltpu.make_async_copy(hold.at[which], outs[which], sems.at[which]))
        stores[-1].start()
    for store in stores:
        store.wait()


def weight_grads(both, pieces, got, width):
    depth = both.shape[2] // 2
    return pl.pallas_call(
        grad_kernel,
        out_shape=[jax.ShapeDtypeStruct((width, depth), jnp.bfloat16)] * 3,
        in_specs=[pl.BlockSpec(memory_space=pltpu.VMEM)] * 3,
        out_specs=[pl.BlockSpec(memory_space=pl.ANY)] * 3,
        scratch_shapes=[
            pltpu.VMEM((3, width, depth), jnp.bfloat16),
            pltpu.SemaphoreType.DMA((3,)),
        ],
        compiler_params=pltpu.CompilerParams(vmem_limit_bytes=16 << 20),
        cost_estimate=pl.CostEstimate(
            flops=24 * both.shape[1] * width * depth, bytes_accessed=4 << 20, transcendentals=0
        ),
        name="weight_grads",
    )(both, pieces, got)


def sum_kernel(blocks, out):
    out[...] = jnp.sum(blocks[...].astype(jnp.float32), axis=0).astype(out.dtype)


def final_sum(blocks):
    return pl.pallas_call(
        sum_kernel,
        out_shape=jax.ShapeDtypeStruct(blocks.shape[1:], jnp.bfloat16),
        in_specs=[pl.BlockSpec(memory_space=pltpu.VMEM)],
        out_specs=pl.BlockSpec(memory_space=pltpu.VMEM),
        compiler_params=pltpu.CompilerParams(vmem_limit_bytes=16 << 20),
        name="final_sum",
    )(blocks)


def on_device(rows, chips, inputs, out_grad, w_gate, w_up, w_down):
    width = w_gate.shape[1]
    own = jnp.zeros((3 * width, w_down.shape[1]), w_down.dtype)
    for i, w in enumerate((w_gate.T, w_up.T, w_down)):
        own = lax.dynamic_update_slice(own, w, (i * width, 0))
    copies = jnp.concatenate([inputs, out_grad], axis=1)
    copies = jnp.broadcast_to(copies[None], (chips, *copies.shape))
    both = lax.all_to_all(copies, "chip", 0, 0).reshape(-1, copies.shape[2])
    theirs = lax.ppermute(own, "core", SWAP)
    partial = fold(*partial_sums(both, own, theirs), rows)
    blocks = exchange(partial.astype(jnp.float16), ROW, rows)
    payload = activations(blocks.astype(jnp.float32))
    pieces = lax.all_gather(payload, ROW, axis=0, tiled=True)
    block_in = block_inputs(pieces, own, theirs)
    block_in, pieces, both = lax.optimization_barrier((block_in, pieces, both))
    block_in = exchange(block_in, "chip", chips)
    got = lax.all_gather(given(pieces), "core", axis=0)
    grads = weight_grads(lax.all_gather(both, "core", axis=0), pieces, got, width)
    block_in, grad_gate, grad_up, grad_down = lax.optimization_barrier((block_in, *grads))
    grad_inputs = final_sum(block_in)
    return (grad_inputs, grad_gate.T, grad_up.T, grad_down)


def solution(mesh):
    rows, cols = mesh.shape["row"], mesh.shape["col"]
    split = Mesh(mesh.devices.reshape(rows // 2, 2, cols // 2, 2), ROW + COL)
    in_specs = (P(COL, ROW), P(COL, ROW), P(ROW, COL), P(ROW, COL), P(COL, ROW))
    out_specs = (P(COL, ROW), P(ROW, COL), P(ROW, COL), P(COL, ROW))

    def step(*arrays):
        return on_device(rows, cols // 2, *arrays)

    return jax.shard_map(
        step, mesh=split, in_specs=in_specs, out_specs=out_specs, check_vma=False
    )
```

```python
import jax
import jax.numpy as jnp
from jax import lax
from jax.experimental import pallas as pl
from jax.experimental.pallas import tpu as pltpu
from jax.sharding import Mesh
from jax.sharding import PartitionSpec as P

ROW = ("far", "pair")
COL = ("chip", "core")
SWAP = [(0, 1), (1, 0)]
LEAST = -100.0
SHIFT = 9.0
PAIR_SHIFT = 8.0
NOTE = 64


def contract(left, right, left_dim, right_dim):
    return lax.dot_general(
        left, right, (((left_dim,), (right_dim,)), ((), ())), preferred_element_type=jnp.float32
    )


def activate(gate, up, hidden_grad):
    sigmoid_gate = jax.nn.sigmoid(gate)
    activated = gate * sigmoid_gate
    hidden = (activated * up).astype(jnp.bfloat16)
    up_delta = (hidden_grad * activated).astype(jnp.bfloat16)
    gate_delta = (hidden_grad * up * sigmoid_gate * (1.0 + gate * (1.0 - sigmoid_gate))).astype(
        jnp.bfloat16
    )
    return (hidden, gate_delta, up_delta)


def exchange(array, axis, pieces):
    return lax.all_to_all(array.reshape(pieces, -1, array.shape[-1]), axis, 0, 0)


def own_kernel(both, own, out):
    width, depth = own.shape[0] // 3, own.shape[1]
    notes = []
    for i, side in enumerate((0, 0, 1)):
        x = both[:, side * depth : (side + 1) * depth]
        if i != 1:
            largest = jnp.max(jnp.abs(x).astype(jnp.float32), axis=0, keepdims=True)
            largest = jnp.max(largest, axis=1, keepdims=True)
            exp = jnp.ceil(jnp.log2(jnp.maximum(largest, 2.0**LEAST)))
            notes.append(jnp.broadcast_to(exp, (out.shape[0], NOTE // 2)))
        at = slice(i * width, (i + 1) * width)
        out[:, at] = contract(x, own[at], 1, 1)
    out[:, 3 * width :] = jnp.concatenate(notes, axis=1)


def other_kernel(both, theirs, firsts, sent, kept):
    depth = theirs.shape[1]
    width = theirs.shape[0] // 3
    same = lax.axis_index("pair") == lax.axis_index("core")
    scales = [jnp.exp2(SHIFT - exp) for exp in exponents(firsts[...])]
    for i, side in enumerate((0, 0, 1)):
        x = both[:, side * depth : (side + 1) * depth]
        at = slice(i * width, (i + 1) * width)
        first = firsts[:, at]
        second = contract(x, theirs[at], 1, 1)
        kept[:, at] = jnp.where(same, first, second)
        sent[:, at] = jnp.where(same, second, first) * scales[side]
    notes = firsts[:, 3 * width :]
    kept[:, 3 * width :] = notes
    sent[:, 3 * width :] = notes


def partial_sums(both, own, theirs):
    tokens, width = both.shape[0], own.shape[0] // 3
    vmem = pl.BlockSpec(memory_space=pltpu.VMEM)
    params = pltpu.CompilerParams(vmem_limit_bytes=16 << 20)
    firsts = pl.pallas_call(
        own_kernel,
        out_shape=jax.ShapeDtypeStruct((tokens, 3 * width + NOTE), jnp.float32),
        in_specs=[vmem] * 2,
        out_specs=vmem,
        compiler_params=params,
        cost_estimate=pl.CostEstimate(flops=10**11, bytes_accessed=3 << 20, transcendentals=0),
        name="own_sums",
    )(both, own)
    return pl.pallas_call(
        other_kernel,
        out_shape=[jax.ShapeDtypeStruct((tokens, 3 * width + NOTE), jnp.float32)] * 2,
        in_specs=[vmem] * 3,
        out_specs=[vmem] * 2,
        compiler_params=params,
        name="other_sums",
    )(both, theirs, firsts)


def exponents(block):
    at = block.shape[-1] - NOTE
    return block[..., at : at + 1], block[..., at + NOTE // 2 : at + NOTE // 2 + 1]


def fold_kernel(got, kept, out):
    parity, core = lax.axis_index("pair"), lax.axis_index("core")
    theirs, mine = got[jnp.where(core == 0, 1 - parity, parity)], kept[...]
    at = mine.shape[1] - NOTE
    column = lax.broadcasted_iota(jnp.int32, (mine.shape[0], at), 1)
    grads = column >= 2 * (at // 3)
    got_in, got_grad = exponents(theirs)
    own_in, own_grad = exponents(mine)
    exp_in, exp_grad = jnp.maximum(got_in, own_in), jnp.maximum(got_grad, own_grad)
    scale = jnp.where(grads, jnp.exp2(got_grad - SHIFT), jnp.exp2(got_in - SHIFT))
    total = mine[:, :at] + theirs[:, :at] * scale
    scale = jnp.where(grads, jnp.exp2(PAIR_SHIFT - exp_grad), jnp.exp2(PAIR_SHIFT - exp_in))
    out[:, :at] = total * scale
    note = (mine.shape[0], NOTE // 2)
    out[:, at:] = jnp.concatenate(
        [jnp.broadcast_to(exp_in, note), jnp.broadcast_to(exp_grad, note)], axis=1
    )


def neighbours(rows):
    return [(2 * z + c, 2 * ((z + (1 if z % 2 == c else -1)) % rows) + c) for z in range(rows) for c in range(2)]


def fold(sent, kept, rows):
    groups = sorted({tuple(sorted(p, key=lambda i: (i - (i % 2) * 2) % (2 * rows))) for p in neighbours(rows)})
    got = lax.all_gather(
        sent.astype(jnp.float16), (*ROW, "core"), axis=0, axis_index_groups=[list(g) for g in groups]
    )
    got = got.astype(jnp.float32)
    return pl.pallas_call(
        fold_kernel,
        out_shape=jax.ShapeDtypeStruct(kept.shape, jnp.float32),
        in_specs=[pl.BlockSpec(memory_space=pltpu.VMEM)] * 2,
        out_specs=pl.BlockSpec(memory_space=pltpu.VMEM),
        compiler_params=pltpu.CompilerParams(vmem_limit_bytes=16 << 20),
        name="fold",
    )(got, kept)


def activate_kernel(blocks, out):
    width = (blocks.shape[2] - NOTE) // 3
    stride = out.shape[2] // 2
    for h in range(2):
        sums = [0.0, 0.0]
        for s in range(h, blocks.shape[0], 2):
            block = blocks[s]
            parts = block[:, : 2 * width], block[:, 2 * width : 3 * width]
            for i, exp in enumerate(exponents(block)):
                sums[i] += parts[i] * jnp.exp2(exp - PAIR_SHIFT)
        hidden, gate_delta, up_delta = activate(sums[0][:, :width], sums[0][:, width:], sums[1])
        pad = jnp.zeros((hidden.shape[0], stride - 3 * width), out.dtype)
        out[0, :, h * stride : (h + 1) * stride] = jnp.concatenate(
            [gate_delta, up_delta, hidden, pad], axis=1
        )


def activations(blocks):
    stride = -(-blocks.shape[2] // 128) * 128
    return pl.pallas_call(
        activate_kernel,
        out_shape=jax.ShapeDtypeStruct((1, blocks.shape[1], 2 * stride), jnp.bfloat16),
        in_specs=[pl.BlockSpec(memory_space=pltpu.VMEM)],
        out_specs=pl.BlockSpec(memory_space=pltpu.VMEM),
        compiler_params=pltpu.CompilerParams(vmem_limit_bytes=16 << 20),
        name="activations",
    )(blocks)


def piece(pieces, which, width):
    return pieces[:, :, which * width : (which + 1) * width].reshape(-1, width)


def of_core(pieces, core):
    stride = pieces.shape[2] // 2
    return pieces[:, :, pl.ds(pl.multiple_of(core * stride, 128), stride)]


def block_kernel(pieces, own, theirs, out):
    width = own.shape[0] // 3
    core = lax.axis_index("core")
    total = 0.0
    for c, weights in ((core, own), (1 - core, theirs)):
        part = of_core(pieces, c)
        total += contract(piece(part, 0, width), weights[:width], 1, 0)
        total += contract(piece(part, 1, width), weights[width : 2 * width], 1, 0)
    out[...] = total.astype(out.dtype)


def block_inputs(pieces, own, theirs):
    return pl.pallas_call(
        block_kernel,
        out_shape=jax.ShapeDtypeStruct(
            (pieces.shape[0] * pieces.shape[1], own.shape[1]), jnp.bfloat16
        ),
        in_specs=[pl.BlockSpec(memory_space=pltpu.VMEM)] * 3,
        out_specs=pl.BlockSpec(memory_space=pltpu.VMEM),
        compiler_params=pltpu.CompilerParams(vmem_limit_bytes=16 << 20),
        name="block_inputs",
    )(pieces, own, theirs)


def give_kernel(pieces, out):
    out[...] = of_core(pieces, 1 - lax.axis_index("core")).reshape(out.shape)


def given(pieces):
    shape = (pieces.shape[0] * pieces.shape[1], pieces.shape[2] // 2)
    return pl.pallas_call(
        give_kernel,
        out_shape=jax.ShapeDtypeStruct(shape, jnp.bfloat16),
        in_specs=[pl.BlockSpec(memory_space=pltpu.VMEM)],
        out_specs=pl.BlockSpec(memory_space=pltpu.VMEM),
        compiler_params=pltpu.CompilerParams(vmem_limit_bytes=16 << 20),
        name="given",
    )(pieces)


def grad_kernel(both, pieces, got, *refs):
    outs, (hold, sems) = refs[:3], refs[3:]
    width, depth = outs[0].shape
    core = lax.axis_index("core")
    mine = of_core(pieces, core)
    stores = []
    for which, side in ((2, 1), (0, 0), (1, 0)):
        units = slice(which * width, (which + 1) * width)
        features = slice(side * depth, (side + 1) * depth)
        delta = jnp.concatenate([piece(mine, which, width), got[1 - core, :, units]], axis=0)
        x = jnp.concatenate([both[core, :, features], both[1 - core, :, features]], axis=0)
        total = contract(delta, x, 0, 0)
        hold[which] = total.astype(hold.dtype)
        stores.append(pltpu.make_async_copy(hold.at[which], outs[which], sems.at[which]))
        stores[-1].start()
    for store in stores:
        store.wait()


def weight_grads(both, pieces, got, width):
    depth = both.shape[2] // 2
    return pl.pallas_call(
        grad_kernel,
        out_shape=[jax.ShapeDtypeStruct((width, depth), jnp.bfloat16)] * 3,
        in_specs=[pl.BlockSpec(memory_space=pltpu.VMEM)] * 3,
        out_specs=[pl.BlockSpec(memory_space=pl.ANY)] * 3,
        scratch_shapes=[
            pltpu.VMEM((3, width, depth), jnp.bfloat16),
            pltpu.SemaphoreType.DMA((3,)),
        ],
        compiler_params=pltpu.CompilerParams(vmem_limit_bytes=16 << 20),
        cost_estimate=pl.CostEstimate(
            flops=24 * both.shape[1] * width * depth, bytes_accessed=4 << 20, transcendentals=0
        ),
        name="weight_grads",
    )(both, pieces, got)


def sum_kernel(blocks, out):
    out[...] = jnp.sum(blocks[...].astype(jnp.float32), axis=0).astype(out.dtype)


def final_sum(blocks):
    return pl.pallas_call(
        sum_kernel,
        out_shape=jax.ShapeDtypeStruct(blocks.shape[1:], jnp.bfloat16),
        in_specs=[pl.BlockSpec(memory_space=pltpu.VMEM)],
        out_specs=pl.BlockSpec(memory_space=pltpu.VMEM),
        compiler_params=pltpu.CompilerParams(vmem_limit_bytes=16 << 20),
        name="final_sum",
    )(blocks)


def on_device(rows, chips, inputs, out_grad, w_gate, w_up, w_down):
    width = w_gate.shape[1]
    own = jnp.zeros((3 * width, w_down.shape[1]), w_down.dtype)
    for i, w in enumerate((w_gate.T, w_up.T, w_down)):
        own = lax.dynamic_update_slice(own, w, (i * width, 0))
    copies = jnp.concatenate([inputs, out_grad], axis=1)
    copies = jnp.broadcast_to(copies[None], (chips, *copies.shape))
    both = lax.all_to_all(copies, "chip", 0, 0).reshape(-1, copies.shape[2])
    theirs = lax.ppermute(own, "core", SWAP)
    partial = fold(*partial_sums(both, own, theirs), rows)
    blocks = exchange(partial.astype(jnp.float16), ROW, rows)
    payload = activations(blocks.astype(jnp.float32))
    pieces = lax.all_gather(payload, ROW, axis=0, tiled=True)
    block_in = block_inputs(pieces, own, theirs)
    block_in, pieces, both = lax.optimization_barrier((block_in, pieces, both))
    block_in = exchange(block_in, "chip", chips)
    got = lax.all_gather(given(pieces), "core", axis=0)
    grads = weight_grads(lax.all_gather(both, "core", axis=0), pieces, got, width)
    block_in, grad_gate, grad_up, grad_down = lax.optimization_barrier((block_in, *grads))
    grad_inputs = final_sum(block_in)
    return (grad_inputs, grad_gate.T, grad_up.T, grad_down)


def solution(mesh):
    rows, cols = mesh.shape["row"], mesh.shape["col"]
    split = Mesh(mesh.devices.reshape(rows // 2, 2, cols // 2, 2), ROW + COL)
    in_specs = (P(COL, ROW), P(COL, ROW), P(ROW, COL), P(ROW, COL), P(COL, ROW))
    out_specs = (P(COL, ROW), P(ROW, COL), P(ROW, COL), P(COL, ROW))

    def step(*arrays):
        return on_device(rows, cols // 2, *arrays)

    return jax.shard_map(
        step, mesh=split, in_specs=in_specs, out_specs=out_specs, check_vma=False
    )
```

```python
import jax
import jax.numpy as jnp
from jax import lax
from jax.experimental import pallas as pl
from jax.experimental.pallas import tpu as pltpu
from jax.sharding import Mesh
from jax.sharding import PartitionSpec as P

ROW = ("far", "pair")
COL = ("chip", "core")
SWAP = [(0, 1), (1, 0)]
LEAST = -100.0
SHIFT = 9.0
PAIR_SHIFT = 8.0
NOTE = 64


def contract(left, right, left_dim, right_dim):
    return lax.dot_general(
        left, right, (((left_dim,), (right_dim,)), ((), ())), preferred_element_type=jnp.float32
    )


def activate(gate, up, hidden_grad):
    sigmoid_gate = jax.nn.sigmoid(gate)
    activated = gate * sigmoid_gate
    hidden = (activated * up).astype(jnp.bfloat16)
    up_delta = (hidden_grad * activated).astype(jnp.bfloat16)
    gate_delta = (hidden_grad * up * sigmoid_gate * (1.0 + gate * (1.0 - sigmoid_gate))).astype(
        jnp.bfloat16
    )
    return (hidden, gate_delta, up_delta)


def exchange(array, axis, pieces):
    return lax.all_to_all(array.reshape(pieces, -1, array.shape[-1]), axis, 0, 0)


def own_kernel(both, own, out):
    width, depth = own.shape[0] // 3, own.shape[1]
    for i, side in enumerate((0, 0, 1)):
        x = both[:, side * depth : (side + 1) * depth]
        at = slice(i * width, (i + 1) * width)
        out[:, at] = contract(x, own[at], 1, 1)


def other_kernel(both, theirs, firsts, sent, kept):
    depth = theirs.shape[1]
    width = theirs.shape[0] // 3
    same = lax.axis_index("pair") == lax.axis_index("core")
    notes = []
    for i, side in enumerate((0, 0, 1)):
        x = both[:, side * depth : (side + 1) * depth]
        if i != 1:
            largest = jnp.max(jnp.abs(x).astype(jnp.float32), axis=0, keepdims=True)
            largest = jnp.max(largest, axis=1, keepdims=True)
            exp = jnp.ceil(jnp.log2(jnp.maximum(largest, 2.0**LEAST)))
            scale = jnp.exp2(SHIFT - exp)
            notes.append(jnp.broadcast_to(exp, (sent.shape[0], NOTE // 2)))
        at = slice(i * width, (i + 1) * width)
        first = firsts[:, at]
        second = contract(x, theirs[at], 1, 1)
        kept[:, at] = jnp.where(same, first, second)
        sent[:, at] = jnp.where(same, second, first) * scale
    notes = jnp.concatenate(notes, axis=1)
    kept[:, 3 * width :] = notes
    sent[:, 3 * width :] = notes


def partial_sums(both, own, theirs):
    tokens, width = both.shape[0], own.shape[0] // 3
    vmem = pl.BlockSpec(memory_space=pltpu.VMEM)
    params = pltpu.CompilerParams(vmem_limit_bytes=16 << 20)
    firsts = pl.pallas_call(
        own_kernel,
        out_shape=jax.ShapeDtypeStruct((tokens, 3 * width), jnp.float32),
        in_specs=[vmem] * 2,
        out_specs=vmem,
        compiler_params=params,
        cost_estimate=pl.CostEstimate(flops=10**11, bytes_accessed=3 << 20, transcendentals=0),
        name="own_sums",
    )(both, own)
    return pl.pallas_call(
        other_kernel,
        out_shape=[jax.ShapeDtypeStruct((tokens, 3 * width + NOTE), jnp.float32)] * 2,
        in_specs=[vmem] * 3,
        out_specs=[vmem] * 2,
        compiler_params=params,
        name="other_sums",
    )(both, theirs, firsts)


def exponents(block):
    at = block.shape[-1] - NOTE
    return block[..., at : at + 1], block[..., at + NOTE // 2 : at + NOTE // 2 + 1]


def fold_kernel(got, kept, out):
    parity, core = lax.axis_index("pair"), lax.axis_index("core")
    theirs, mine = got[jnp.where(core == 0, 1 - parity, parity)], kept[...]
    at = mine.shape[1] - NOTE
    column = lax.broadcasted_iota(jnp.int32, (mine.shape[0], at), 1)
    grads = column >= 2 * (at // 3)
    got_in, got_grad = exponents(theirs)
    own_in, own_grad = exponents(mine)
    exp_in, exp_grad = jnp.maximum(got_in, own_in), jnp.maximum(got_grad, own_grad)
    scale = jnp.where(grads, jnp.exp2(got_grad - SHIFT), jnp.exp2(got_in - SHIFT))
    total = mine[:, :at] + theirs[:, :at] * scale
    scale = jnp.where(grads, jnp.exp2(PAIR_SHIFT - exp_grad), jnp.exp2(PAIR_SHIFT - exp_in))
    out[:, :at] = total * scale
    note = (mine.shape[0], NOTE // 2)
    out[:, at:] = jnp.concatenate(
        [jnp.broadcast_to(exp_in, note), jnp.broadcast_to(exp_grad, note)], axis=1
    )


def neighbours(rows):
    return [(2 * z + c, 2 * ((z + (1 if z % 2 == c else -1)) % rows) + c) for z in range(rows) for c in range(2)]


def fold(sent, kept, rows):
    groups = sorted({tuple(sorted(p, key=lambda i: (i - (i % 2) * 2) % (2 * rows))) for p in neighbours(rows)})
    got = lax.all_gather(
        sent.astype(jnp.float16), (*ROW, "core"), axis=0, axis_index_groups=[list(g) for g in groups]
    )
    got = got.astype(jnp.float32)
    return pl.pallas_call(
        fold_kernel,
        out_shape=jax.ShapeDtypeStruct(kept.shape, jnp.float32),
        in_specs=[pl.BlockSpec(memory_space=pltpu.VMEM)] * 2,
        out_specs=pl.BlockSpec(memory_space=pltpu.VMEM),
        compiler_params=pltpu.CompilerParams(vmem_limit_bytes=16 << 20),
        name="fold",
    )(got, kept)


def activate_kernel(blocks, out):
    width = (blocks.shape[2] - NOTE) // 3
    stride = out.shape[2] // 2
    for h in range(2):
        sums = [0.0, 0.0]
        for s in range(h, blocks.shape[0], 2):
            block = blocks[s]
            parts = block[:, : 2 * width], block[:, 2 * width : 3 * width]
            for i, exp in enumerate(exponents(block)):
                sums[i] += parts[i] * jnp.exp2(exp - PAIR_SHIFT)
        hidden, gate_delta, up_delta = activate(sums[0][:, :width], sums[0][:, width:], sums[1])
        pad = jnp.zeros((hidden.shape[0], stride - 3 * width), out.dtype)
        out[0, :, h * stride : (h + 1) * stride] = jnp.concatenate(
            [gate_delta, up_delta, hidden, pad], axis=1
        )


def activations(blocks):
    stride = -(-blocks.shape[2] // 128) * 128
    return pl.pallas_call(
        activate_kernel,
        out_shape=jax.ShapeDtypeStruct((1, blocks.shape[1], 2 * stride), jnp.bfloat16),
        in_specs=[pl.BlockSpec(memory_space=pltpu.VMEM)],
        out_specs=pl.BlockSpec(memory_space=pltpu.VMEM),
        compiler_params=pltpu.CompilerParams(vmem_limit_bytes=16 << 20),
        name="activations",
    )(blocks)


def piece(pieces, which, width):
    return pieces[:, :, which * width : (which + 1) * width].reshape(-1, width)


def of_core(pieces, core):
    stride = pieces.shape[2] // 2
    return pieces[:, :, pl.ds(pl.multiple_of(core * stride, 128), stride)]


def block_kernel(pieces, own, theirs, out, given):
    width = own.shape[0] // 3
    core = lax.axis_index("core")
    given[...] = of_core(pieces, 1 - core).reshape(given.shape)
    total = 0.0
    for c, weights in ((core, own), (1 - core, theirs)):
        part = of_core(pieces, c)
        total += contract(piece(part, 0, width), weights[:width], 1, 0)
        total += contract(piece(part, 1, width), weights[width : 2 * width], 1, 0)
    out[...] = total.astype(out.dtype)


def block_inputs(pieces, own, theirs):
    return pl.pallas_call(
        block_kernel,
        out_shape=[
            jax.ShapeDtypeStruct((pieces.shape[0] * pieces.shape[1], columns), jnp.bfloat16)
            for columns in (own.shape[1], pieces.shape[2] // 2)
        ],
        in_specs=[pl.BlockSpec(memory_space=pltpu.VMEM)] * 3,
        out_specs=[pl.BlockSpec(memory_space=pltpu.VMEM)] * 2,
        compiler_params=pltpu.CompilerParams(vmem_limit_bytes=16 << 20),
        name="block_inputs",
    )(pieces, own, theirs)


def grad_kernel(both, pieces, got, *refs):
    outs, (hold, sems) = refs[:3], refs[3:]
    width, depth = outs[0].shape
    core = lax.axis_index("core")
    mine = of_core(pieces, core)
    stores = []
    for which, side in ((2, 1), (0, 0), (1, 0)):
        units = slice(which * width, (which + 1) * width)
        features = slice(side * depth, (side + 1) * depth)
        delta = jnp.concatenate([piece(mine, which, width), got[1 - core, :, units]], axis=0)
        x = jnp.concatenate([both[core, :, features], both[1 - core, :, features]], axis=0)
        total = contract(delta, x, 0, 0)
        hold[which] = total.astype(hold.dtype)
        stores.append(pltpu.make_async_copy(hold.at[which], outs[which], sems.at[which]))
        stores[-1].start()
    for store in stores:
        store.wait()


def weight_grads(both, pieces, got, width):
    depth = both.shape[2] // 2
    return pl.pallas_call(
        grad_kernel,
        out_shape=[jax.ShapeDtypeStruct((width, depth), jnp.bfloat16)] * 3,
        in_specs=[pl.BlockSpec(memory_space=pltpu.VMEM)] * 3,
        out_specs=[pl.BlockSpec(memory_space=pl.ANY)] * 3,
        scratch_shapes=[
            pltpu.VMEM((3, width, depth), jnp.bfloat16),
            pltpu.SemaphoreType.DMA((3,)),
        ],
        compiler_params=pltpu.CompilerParams(vmem_limit_bytes=16 << 20),
        cost_estimate=pl.CostEstimate(
            flops=24 * both.shape[1] * width * depth, bytes_accessed=4 << 20, transcendentals=0
        ),
        name="weight_grads",
    )(both, pieces, got)


def sum_kernel(blocks, out):
    out[...] = jnp.sum(blocks[...].astype(jnp.float32), axis=0).astype(out.dtype)


def final_sum(blocks):
    return pl.pallas_call(
        sum_kernel,
        out_shape=jax.ShapeDtypeStruct(blocks.shape[1:], jnp.bfloat16),
        in_specs=[pl.BlockSpec(memory_space=pltpu.VMEM)],
        out_specs=pl.BlockSpec(memory_space=pltpu.VMEM),
        compiler_params=pltpu.CompilerParams(vmem_limit_bytes=16 << 20),
        name="final_sum",
    )(blocks)


def on_device(rows, chips, inputs, out_grad, w_gate, w_up, w_down):
    width = w_gate.shape[1]
    own = jnp.zeros((3 * width, w_down.shape[1]), w_down.dtype)
    for i, w in enumerate((w_gate.T, w_up.T, w_down)):
        own = lax.dynamic_update_slice(own, w, (i * width, 0))
    copies = jnp.concatenate([inputs, out_grad], axis=1)
    copies = jnp.broadcast_to(copies[None], (chips, *copies.shape))
    both = lax.all_to_all(copies, "chip", 0, 0).reshape(-1, copies.shape[2])
    theirs = lax.ppermute(own, "core", SWAP)
    partial = fold(*partial_sums(both, own, theirs), rows)
    blocks = exchange(partial.astype(jnp.float16), ROW, rows)
    payload = activations(blocks.astype(jnp.float32))
    pieces = lax.all_gather(payload, ROW, axis=0, tiled=True)
    block_in, given = block_inputs(pieces, own, theirs)
    block_in, given, both = lax.optimization_barrier((block_in, given, both))
    block_in = exchange(block_in, "chip", chips)
    got = lax.all_gather(given, "core", axis=0)
    grads = weight_grads(lax.all_gather(both, "core", axis=0), pieces, got, width)
    block_in, grad_gate, grad_up, grad_down = lax.optimization_barrier((block_in, *grads))
    grad_inputs = final_sum(block_in)
    return (grad_inputs, grad_gate.T, grad_up.T, grad_down)


def solution(mesh):
    rows, cols = mesh.shape["row"], mesh.shape["col"]
    split = Mesh(mesh.devices.reshape(rows // 2, 2, cols // 2, 2), ROW + COL)
    in_specs = (P(COL, ROW), P(COL, ROW), P(ROW, COL), P(ROW, COL), P(COL, ROW))
    out_specs = (P(COL, ROW), P(ROW, COL), P(ROW, COL), P(COL, ROW))

    def step(*arrays):
        return on_device(rows, cols // 2, *arrays)

    return jax.shard_map(
        step, mesh=split, in_specs=in_specs, out_specs=out_specs, check_vma=False
    )
```
